32 devices in a mesh: energy: 2 (over x), atom: 4 (over y, core), orb: 4 (over z).
Axes of the slice: x: 2, y: 2, z: 4, core: 2. Of those that a mesh axis runs over, the one named last changes fastest.
Arguments:
- green_lesser: bfloat16 [8, 4, 64, 128], P(('energy', 'atom'), None, 'orb'), may hold values from -6 to 6
- occupation: float32 [2], replicated, may hold values from 0.1 to 2
- coupling_blocks: bfloat16 [32, 2, 64, 64], replicated, may hold values from -0.375 to 0.375
- neighbours: int32 [4, 8], P('atom'), may hold values from 0 to 3, as said below
- coupling_index: int32 [4, 8], P('atom'), may hold values from 0 to 31
- neighbour_count: int32 [4], P('atom'), may hold values from 2 to 8, as said below
Outputs:
- sigma_lesser: bfloat16 [8, 4, 64, 128], P(('energy', 'atom'), None, 'orb')
The draws below stay inside these ranges and needn't reach their ends.
Inputs may be any that keep to these rules, and one draw needn't show every extreme that they name: `neighbours`: row a lists atoms at most 1 positions from atom a; repeats are allowed. Slots p with p >= neighbour_count[a] are unused.
All inputs are finite; a program needn't handle non-finite values.
Results may differ from the reference program's by a relative error of at most 0.0057.
Values may be sent and summed in bfloat16 or wider, within the bound.
No kernel may reach another device: no remote copies, remote signals or barrier semaphores. Data moves between devices by JAX's collectives and lax.ppermute only.
A program may use at most 64 MiB of HBM per device.

```python
import math
import jax
import jax.numpy as jnp
from jax import lax

ORB = 64
MODES = 2
SHIFT_LO = 2
SHIFT_HI = 4
NB_MAX = 8
NCOUP = 32
A_DEV = 1
NA = 4
NE = 8


def draw_neighbours(key, part):
    offsets = jax.random.randint(key, (NA, NB_MAX), -A_DEV, A_DEV + 1)
    atom_rows = lax.broadcasted_iota(jnp.int32, (NA, NB_MAX), 0)
    slot_rows = lax.broadcasted_iota(jnp.int32, (NA, NB_MAX), 1)
    offsets = jnp.where(slot_rows == 0, -A_DEV, offsets)
    offsets = jnp.where(slot_rows == 1, A_DEV, offsets)
    chosen = jnp.clip(atom_rows + offsets, 0, NA - 1)
    return chosen.astype(jnp.int32)


def draw_neighbour_count(key, part):
    first_key = jax.random.fold_in(key, 11)
    second_key = jax.random.fold_in(key, 12)
    drawn_counts = jax.random.randint(first_key, (NA,), 2, NB_MAX + 1)
    fullest = jax.random.randint(second_key, (), 0, NA)
    emptiest = (fullest + 1) % NA
    positions = lax.broadcasted_iota(jnp.int32, (NA,), 0)
    counts = jnp.where(positions == emptiest, 2, drawn_counts)
    return jnp.where(positions == fullest, NB_MAX, counts).astype(jnp.int32)


def set_ends(array, key, least, top_value):
    spot = [jax.random.randint(jax.random.fold_in(key, axis), (), 0, length) for axis, length in enumerate(array.shape)]
    main_axis = array.shape.index(max(array.shape))
    next_to = spot[:main_axis] + [(spot[main_axis] + 1) % array.shape[main_axis]] + spot[main_axis + 1:]
    return array.at[tuple(spot)].set(least).at[tuple(next_to)].set(top_value)


def steps_of(stream_key, extent, cuts, low, largest):
    def one(axis_at, shards_of):
        steps = jax.random.uniform(jax.random.fold_in(jax.random.fold_in(stream_key, 6), axis_at), (shards_of,), jnp.float32, low / len(cuts), largest / len(cuts))
        return jnp.repeat(jnp.exp(steps), extent[axis_at] // shards_of).reshape((-1,) + (1,) * (len(extent) - axis_at - 1))

    loudness = one(*cuts[0])
    for cut in cuts[1:]:
        loudness = loudness * one(*cut)
    return loudness


def bell_draw(own_key, shape, spread, bound, pieces=(), kind=jnp.bfloat16):
    values = spread * jax.random.normal(own_key, shape, jnp.float32)
    if pieces:
        values = values * steps_of(own_key, shape, pieces, -0.22, 0.18)
    return jnp.clip(values, -bound, bound).astype(kind)


def setup_inputs(seed: int = 0) -> dict:
    splits = jax.random.split(jax.random.key(seed), 7)
    green_lesser = bell_draw(splits[0], (NE, NA, ORB, 2 * ORB), 1.0, 6.0, ((0, 8), (2, 4)))
    occupation = jnp.clip(jnp.exp(jax.random.uniform(splits[1], (MODES,), jnp.float32, math.log(0.1), math.log(2.0))), 0.1, 2.0)
    coupling_blocks = bell_draw(splits[2], (NCOUP, MODES, ORB, ORB), (4 * ORB) ** -0.5, 0.375)
    neighbours = draw_neighbours(jax.random.fold_in(splits[6], 71), 0)
    coupling_index = set_ends(jax.random.randint(splits[4], (NA, NB_MAX), 0, NCOUP), jax.random.fold_in(splits[4], 1), 0, NCOUP - 1).astype(jnp.int32)
    neighbour_count = draw_neighbour_count(jax.random.fold_in(splits[6], 71), 0)
    return {"green_lesser": green_lesser, "occupation": occupation, "coupling_blocks": coupling_blocks, "neighbours": neighbours, "coupling_index": coupling_index, "neighbour_count": neighbour_count}


def reference(green_lesser, occupation, coupling_blocks, neighbours, coupling_index, neighbour_count):
    energy_count = green_lesser.shape[0]
    atom_count, slot_count = neighbours.shape
    orbital = coupling_blocks.shape[-1]
    couplings = jnp.take(coupling_blocks, coupling_index, axis=0).astype(jnp.float32)
    slot_index = lax.broadcasted_iota(jnp.int32, (atom_count, slot_count), 1)
    weights = (slot_index < neighbour_count[:, None]).astype(jnp.float32)

    def fetch_level(level):
        inside = jnp.logical_and(level >= 0, level < energy_count)
        clipped = jnp.clip(level, 0, energy_count - 1).astype(jnp.int32)
        energy_block = lax.dynamic_index_in_dim(green_lesser, clipped, 0, keepdims=False)
        energy_block = jnp.take(energy_block, neighbours, axis=0).astype(jnp.float32)
        return jnp.where(inside, energy_block, jnp.zeros_like(energy_block))

    def one_energy(level):
        running = jnp.zeros((atom_count, orbital, 2 * orbital), jnp.float32)
        for phonon, shift_size in enumerate((SHIFT_LO, SHIFT_HI)):
            below_rows = fetch_level(level - shift_size)
            above_rows = fetch_level(level + shift_size)
            combined = (occupation[phonon] * below_rows + (occupation[phonon] + 1.0) * above_rows) * weights[:, :, None, None]
            combined = lax.optimization_barrier(combined.astype(jnp.bfloat16)).astype(jnp.float32)
            matrices = couplings[:, :, phonon]
            left_product = jnp.einsum("apjck,apik->apjci", combined.reshape(atom_count, slot_count, orbital, 2, orbital), matrices)
            left_product = lax.optimization_barrier(left_product.astype(jnp.bfloat16)).astype(jnp.float32)
            left_product = left_product.reshape(atom_count, slot_count, orbital, 2 * orbital)
            running = running + jnp.einsum("aplj,apjx->alx", matrices, left_product)
        return running.astype(jnp.bfloat16)

    return lax.map(one_energy, jnp.arange(energy_count, dtype=jnp.int32))
```

```python
import functools
import math

import jax
import jax.numpy as jnp
from jax import lax
from jax.experimental import pallas as pl
from jax.experimental.pallas import tpu as pltpu
from jax.sharding import PartitionSpec as P

SHIFTS = (2, 4)
A_DEV = 1
EA = ("energy", "atom")
ALL = ("energy", "atom", "orb")


def combine(blocks_ref, low, high, low_scale, high_scale, atom):
    below = blocks_ref[low, :, atom].astype(jnp.float32)
    above = blocks_ref[high, :, atom].astype(jnp.float32)
    mixed = (low_scale * below + high_scale * above).astype(jnp.bfloat16)
    return mixed.reshape(-1, mixed.shape[-1])


def sigma_kernel(dense, spacing, nbr_ref, index_ref, count_ref, occ_ref, blocks_ref, couplings_ref, out_ref, mixed_ref):
    atoms, slots = nbr_ref.shape
    energies = blocks_ref.shape[0]
    rows = blocks_ref.shape[3]
    orbital = couplings_ref.shape[-1]
    row_start = pl.multiple_of(lax.axis_index("orb") * rows, rows)
    own = (lax.axis_index("energy") * lax.axis_size("atom") + lax.axis_index("atom")) // spacing

    def side(mode, sign):
        if not dense:
            return 2 * mode + (sign + 1) // 2, jnp.float32(1.0)
        at = own + sign * (SHIFTS[mode] // spacing)
        inside = jnp.logical_and(at >= 0, at < energies)
        return jnp.clip(at, 0, energies - 1), jnp.where(inside, jnp.float32(1.0), jnp.float32(0.0))

    sides = []
    for mode in range(len(SHIFTS)):
        low, low_in = side(mode, -1)
        high, high_in = side(mode, 1)
        occ = occ_ref[mode]
        sides.append((low, high, occ * low_in, (occ + 1.0) * high_in))

    def store_mixed(atom):
        empty = jnp.zeros((orbital, 2 * orbital), jnp.bfloat16)
        first, second = [combine(blocks_ref, *sides[m], atom) for m in range(2)]
        mixed_ref[atom + A_DEV] = jnp.concatenate(
            [jnp.concatenate([first, empty], 1), jnp.concatenate([empty, second], 1)], 0
        )

    def one_atom(atom, window):
        lhs, matrices = [], []
        for p in range(slots):
            block = index_ref[atom, p]
            matrices.append(jnp.concatenate([couplings_ref[block, 0], couplings_ref[block, 1]], 1))
            part = jnp.concatenate(
                [couplings_ref[block, m, pl.ds(row_start, rows), :] for m in range(2)], 1
            )
            used = p < count_ref[atom]
            named = nbr_ref[atom, p] - atom
            lhs.append(
                jnp.concatenate(
                    [
                        jnp.where(jnp.logical_and(used, named == d), part, jnp.zeros_like(part))
                        for d in window
                    ],
                    1,
                )
            )
        lhs = jnp.concatenate(lhs, 0)
        rhs = jnp.concatenate([mixed_ref[atom + d + A_DEV] for d in window], 0)
        half = jnp.dot(lhs, rhs, preferred_element_type=jnp.float32).astype(jnp.bfloat16)
        parts = []
        for c in range(2):
            z = jnp.concatenate(
                [half[:, (2 * m + c) * orbital : (2 * m + c + 1) * orbital] for m in range(2)], 1
            )
            parts.append(jnp.concatenate([z[p * rows : (p + 1) * rows] for p in range(slots)], 1))
        total = lax.dot_general(
            jnp.concatenate(parts, 0),
            jnp.concatenate(matrices, 1),
            (((1,), (1,)), ((), ())),
            preferred_element_type=jnp.float32,
        )
        out_ref[0, atom] = jnp.concatenate([total[:rows], total[rows:]], 1).astype(out_ref.dtype)

    if atoms <= 8:
        for atom in range(atoms):
            store_mixed(atom)
        for atom in range(atoms):
            one_atom(atom, [d for d in range(-A_DEV, A_DEV + 1) if 0 <= atom + d < atoms])
    else:
        for edge in list(range(A_DEV)) + list(range(atoms + A_DEV, atoms + 2 * A_DEV)):
            mixed_ref[edge] = jnp.zeros(mixed_ref.shape[1:], mixed_ref.dtype)
        pl.loop(0, atoms)(store_mixed)
        pl.loop(0, atoms)(lambda atom: one_atom(atom, range(-A_DEV, A_DEV + 1)))


def gathered_blocks(green, energies, spacing, orb):
    if energies <= 2 * max(SHIFTS):
        groups = [
            [e * orb + o for e in range(c, energies, spacing) for o in range(orb)]
            for c in range(spacing)
        ]
        copies = jnp.broadcast_to(green, (len(groups[0]),) + green.shape[1:])
        got = lax.all_to_all(copies, ALL, 0, 0, axis_index_groups=groups, tiled=True)
        return True, got.reshape((energies // spacing, orb) + green.shape[1:])
    shares = lax.all_gather(green[0], "orb")
    got = [
        lax.ppermute(shares, EA, [(e, e - s) for e in range(energies) if 0 <= e - s < energies])
        for shift in SHIFTS
        for s in (-shift, shift)
    ]
    return False, jnp.stack(got)


def body(energies, orb, green_lesser, occupation, coupling_blocks, neighbours, coupling_index, neighbour_count):
    spacing = math.gcd(*SHIFTS)
    dense, blocks = gathered_blocks(green_lesser, energies, spacing, orb)
    slots = neighbours.shape[1]
    table = jnp.concatenate([neighbours, coupling_index, neighbour_count[:, None]], 1)
    table = lax.all_gather(table, "atom", tiled=True)
    atoms = table.shape[0]
    orbital = coupling_blocks.shape[-1]
    smem = pl.BlockSpec(memory_space=pltpu.SMEM)
    vmem = pl.BlockSpec(memory_space=pltpu.VMEM)
    return pl.pallas_call(
        functools.partial(sigma_kernel, dense, spacing),
        out_shape=jax.ShapeDtypeStruct(green_lesser.shape, green_lesser.dtype),
        in_specs=[smem, smem, smem, smem, vmem, vmem],
        out_specs=vmem,
        scratch_shapes=[pltpu.VMEM((atoms + 2 * A_DEV, 2 * orbital, 4 * orbital), jnp.bfloat16)],
        compiler_params=pltpu.CompilerParams(vmem_limit_bytes=32 * 1024 * 1024),
    )(
        table[:, :slots],
        table[:, slots : 2 * slots],
        table[:, 2 * slots],
        occupation,
        blocks,
        coupling_blocks,
    )


def solution(mesh):
    orb = mesh.shape["orb"]
    energies = mesh.shape["energy"] * mesh.shape["atom"]
    placed = (
        P(EA, None, "orb", None),
        P(),
        P(),
        P("atom", None),
        P("atom", None),
        P("atom"),
    )
    return jax.shard_map(
        functools.partial(body, energies, orb),
        mesh=mesh,
        in_specs=placed,
        out_specs=P(EA, None, "orb", None),
        check_vma=False,
    )
```

```python
import functools
import math

import jax
import jax.numpy as jnp
from jax import lax
from jax.experimental import pallas as pl
from jax.experimental.pallas import tpu as pltpu
from jax.sharding import PartitionSpec as P

SHIFTS = (2, 4)
MODES = len(SHIFTS)
A_DEV = 1
WINDOW = range(-A_DEV, A_DEV + 1)
EA = ("energy", "atom")
ALL = ("energy", "atom", "orb")
SMEM = pl.BlockSpec(memory_space=pltpu.SMEM)
VMEM = pl.BlockSpec(memory_space=pltpu.VMEM)
ANY = pl.BlockSpec(memory_space=pl.ANY)
VMEM_LIMIT = 32 * 1024 * 1024


def in_hbm(array):
    return pltpu.with_memory_space_constraint(array, pltpu.HBM)


def each_atom(atoms, step):
    if atoms <= 8:
        for atom in range(atoms):
            step(atom)
    else:
        pl.loop(0, atoms)(step)


def copies_kernel(green_ref, couplings_ref, copies_ref, held_ref, own_ref, sems):
    members = copies_ref.shape[0]
    own = pltpu.make_async_copy(green_ref.at[0], own_ref, sems.at[members])
    own.start()
    fetch = pltpu.make_async_copy(couplings_ref, held_ref, sems.at[members + 1])
    fetch.start()
    own.wait()
    copies = [
        pltpu.make_async_copy(own_ref, copies_ref.at[k], sems.at[k]) for k in range(members)
    ]
    for copy in copies:
        copy.start()
    for copy in [*copies, fetch]:
        copy.wait()


def energy_position(spacing):
    return (lax.axis_index("energy") * lax.axis_size("atom") + lax.axis_index("atom")) // spacing


def prepare_kernel(peers, positions, spacing, *refs):
    *tables, occ_ref, couplings_ref, left_ref, stack_ref, factor_ref = refs
    for mode, shift in enumerate(SHIFTS):
        for k, sign in enumerate((-1, 1)):
            factor = occ_ref[mode] + float(k)
            if positions:
                at = energy_position(spacing) + sign * (shift // spacing)
                factor = jnp.where(jnp.logical_and(at >= 0, at < positions), factor, 0.0)
            factor_ref[2 * mode + k] = jnp.full(factor_ref.shape[1:], factor, jnp.float32)
    slots = stack_ref.shape[2] // (2 * couplings_ref.shape[-1])
    rows = left_ref.shape[1] // slots
    lanes = MODES * couplings_ref.shape[-1]
    row_start = pl.multiple_of(lax.axis_index("orb") * rows, rows)

    def prepare(atom, entry):
        count = entry(2, 0)
        for p in range(slots):
            block = entry(1, p)
            stack_ref[atom, :, p * lanes : (p + 1) * lanes] = jnp.concatenate(
                [couplings_ref[block, m] for m in range(MODES)], 1
            )
            part = jnp.concatenate(
                [couplings_ref[block, m, pl.ds(row_start, rows), :] for m in range(MODES)], 1
            )
            place = jnp.where(p < count, entry(0, p) - atom, A_DEV + 1)
            for k, d in enumerate(WINDOW):
                left_ref[atom, p * rows : (p + 1) * rows, k * lanes : (k + 1) * lanes] = jnp.where(
                    place == d, part, jnp.zeros_like(part)
                )

    if peers:
        me = lax.axis_index("atom")
        for k, table_ref in enumerate(tables):
            prepare(me ^ k, lambda row, p, t=table_ref: t[row, p])
    else:
        (table_ref,) = tables
        pl.loop(0, left_ref.shape[0])(lambda a: prepare(a, lambda row, p: table_ref[a, row, p]))


def sigma_kernel(dense, spacing, factor_ref, blocks_ref, left_ref, stack_ref, out_ref, mixed_ref):
    energies, shares, atoms, rows, _ = blocks_ref.shape
    orbital = rows * shares
    slots = left_ref.shape[1] // rows
    lanes = MODES * orbital

    def place(mode, k):
        if not dense:
            return 2 * mode + k
        at = energy_position(spacing) + (2 * k - 1) * (SHIFTS[mode] // spacing)
        return jnp.clip(at, 0, energies - 1)

    sides = [
        (place(m, 0), place(m, 1), factor_ref[2 * m], factor_ref[2 * m + 1]) for m in range(MODES)
    ]

    def combine(atom):
        empty = jnp.zeros((orbital, 2 * orbital), jnp.bfloat16)
        mixed = []
        for low, high, low_scale, high_scale in sides:
            parts = [
                (
                    low_scale * blocks_ref[low, o, atom].astype(jnp.float32)
                    + high_scale * blocks_ref[high, o, atom].astype(jnp.float32)
                ).astype(jnp.bfloat16)
                for o in (range(shares - 1, -1, -1) if dense else range(shares))
            ]
            mixed.append(jnp.concatenate(parts, 0))
        mixed_ref[atom + A_DEV] = jnp.concatenate(
            [jnp.concatenate([mixed[0], empty], 1), jnp.concatenate([empty, mixed[1]], 1)], 0
        )

    def one_atom(atom):
        window = [d for d in WINDOW if atoms > 8 or 0 <= atom + d < atoms]
        first, last = window[0] + A_DEV, window[-1] + A_DEV + 1
        rhs = jnp.concatenate([mixed_ref[atom + d + A_DEV] for d in window], 0)
        half = jnp.dot(
            left_ref[atom, :, first * lanes : last * lanes], rhs, preferred_element_type=jnp.float32
        ).astype(jnp.bfloat16)
        parts = []
        for c in range(2):
            z = jnp.concatenate(
                [half[:, (2 * m + c) * orbital : (2 * m + c + 1) * orbital] for m in range(MODES)], 1
            )
            parts.append(jnp.concatenate([z[p * rows : (p + 1) * rows] for p in range(slots)], 1))
        total = lax.dot_general(
            jnp.concatenate(parts, 0),
            stack_ref[atom],
            (((1,), (1,)), ((), ())),
            preferred_element_type=jnp.float32,
        )
        out_ref[0, atom] = jnp.concatenate([total[:rows], total[rows:]], 1).astype(out_ref.dtype)

    if atoms > 8:
        for edge in list(range(A_DEV)) + list(range(atoms + A_DEV, atoms + 2 * A_DEV)):
            mixed_ref[edge] = jnp.zeros(mixed_ref.shape[1:], mixed_ref.dtype)
    each_atom(atoms, combine)
    each_atom(atoms, one_atom)


def body(energies, orb, green_lesser, occupation, coupling_blocks, neighbours, coupling_index, neighbour_count):
    spacing = math.gcd(*SHIFTS)
    _, atoms, rows, width = green_lesser.shape
    slots = neighbours.shape[1]
    orbital = coupling_blocks.shape[-1]
    lanes = MODES * orbital
    peers = lax.axis_size("atom")
    dense = energies <= 2 * max(SHIFTS)
    swap = peers <= 4 and peers & (peers - 1) == 0 and peers == atoms
    params = pltpu.CompilerParams(vmem_limit_bytes=VMEM_LIMIT)

    groups = [
        [e * orb + o for e in range(c, energies, spacing) for o in range(orb - 1, -1, -1)]
        for c in range(spacing)
    ]
    members = len(groups[0]) if dense else 1
    copies, couplings = pl.pallas_call(
        copies_kernel,
        out_shape=(
            jax.ShapeDtypeStruct((members, atoms, rows, width), green_lesser.dtype),
            pltpu.VMEM(coupling_blocks.shape, coupling_blocks.dtype),
        ),
        in_specs=[ANY, ANY],
        out_specs=(ANY, VMEM),
        scratch_shapes=[
            pltpu.VMEM((atoms, rows, width), green_lesser.dtype),
            pltpu.SemaphoreType.DMA((members + 2,)),
        ],
        compiler_params=params,
    )(in_hbm(green_lesser), in_hbm(coupling_blocks))
    table = jnp.concatenate(
        [neighbours, coupling_index, jnp.broadcast_to(neighbour_count[:, None], (1, slots))], 0
    )

    if dense:
        got = lax.all_to_all(copies, ALL, 0, 0, axis_index_groups=groups, tiled=True)
        blocks = got.reshape(energies // spacing, orb, atoms, rows, width)
    else:
        shares = lax.all_gather(green_lesser[0], "orb")
        blocks = jnp.stack(
            [
                lax.ppermute(shares, EA, [(e, e - s) for e in range(energies) if 0 <= e - s < energies])
                for shift in SHIFTS
                for s in (-shift, shift)
            ]
        )
    if swap:
        tables = [table] + [
            lax.ppermute(table, "atom", [(i, i ^ k) for i in range(peers)]) for k in range(1, peers)
        ]
    else:
        tables = [lax.all_gather(table, "atom")]

    left, stack, factors = pl.pallas_call(
        functools.partial(
            prepare_kernel, peers if swap else 0, energies // spacing if dense else 0, spacing
        ),
        out_shape=(
            jax.ShapeDtypeStruct((atoms, slots * rows, len(WINDOW) * lanes), jnp.bfloat16),
            jax.ShapeDtypeStruct((atoms, orbital, slots * lanes), jnp.bfloat16),
            jax.ShapeDtypeStruct((2 * MODES, rows, width), jnp.float32),
        ),
        in_specs=[SMEM] * (len(tables) + 1) + [VMEM],
        out_specs=(VMEM, VMEM, VMEM),
        compiler_params=params,
    )(*tables, occupation, couplings)

    return pl.pallas_call(
        functools.partial(sigma_kernel, dense, spacing),
        out_shape=jax.ShapeDtypeStruct(green_lesser.shape, green_lesser.dtype),
        in_specs=[VMEM] * 4,
        out_specs=VMEM,
        scratch_shapes=[pltpu.VMEM((atoms + 2 * A_DEV, lanes, 2 * lanes), jnp.bfloat16)],
        compiler_params=params,
    )(factors, blocks, left, stack)


def solution(mesh):
    orb = mesh.shape["orb"]
    energies = mesh.shape["energy"] * mesh.shape["atom"]
    placed = (
        P(EA, None, "orb", None),
        P(),
        P(),
        P("atom", None),
        P("atom", None),
        P("atom"),
    )
    return jax.shard_map(
        functools.partial(body, energies, orb),
        mesh=mesh,
        in_specs=placed,
        out_specs=P(EA, None, "orb", None),
        check_vma=False,
    )
```

```python
import functools
import math

import jax
import jax.numpy as jnp
from jax import lax
from jax.experimental import pallas as pl
from jax.experimental.pallas import tpu as pltpu
from jax.sharding import PartitionSpec as P

SHIFTS = (2, 4)
MODES = len(SHIFTS)
A_DEV = 1
EA = ("energy", "atom")
ALL = ("energy", "atom", "orb")
SMEM = pl.BlockSpec(memory_space=pltpu.SMEM)
VMEM = pl.BlockSpec(memory_space=pltpu.VMEM)
ANY = pl.BlockSpec(memory_space=pl.ANY)
VMEM_LIMIT = 32 * 1024 * 1024
MEASURED = (
    (14, 3, 2, 0, 7, 6, 5, 4, 9, 10, 8, 1, 11, 15, 13, 12),
    (3, 2, 1, 0, 7, 11, 4, 6, 8, 10, 15, 5, 9, 14, 13, 12),
)
FEW = 4


def group_orders(energies, spacing, orb):
    if (energies, spacing, orb) == (8, 2, 4):
        return MEASURED
    return (tuple(range(energies // spacing * orb)),) * spacing


def member_place(orders, orb, own_group, energy, share):
    energies = len(orders[0]) // orb
    if energies * len(orders) > 8 or len(orders[0]) > 16:
        return energy * orb + share
    packed = 0
    for g, order in enumerate(orders):
        for e in range(energies):
            packed |= order.index(e * orb + share) << 4 * (g * energies + e)
    packed -= (packed >> 31) << 32
    shift = 4 * (own_group * energies + energy)
    return lax.shift_right_logical(jnp.int32(packed), shift.astype(jnp.int32)) & 15


def in_hbm(array):
    return pltpu.with_memory_space_constraint(array, pltpu.HBM)


def copies_kernel(green_ref, nbr_ref, index_ref, copies_ref, table_ref, own_ref, sems):
    members = copies_ref.shape[0]
    own = pltpu.make_async_copy(green_ref.at[0], own_ref, sems.at[members])
    lists = [
        pltpu.make_async_copy(ref, table_ref.at[k : k + 1], sems.at[members + 1 + k])
        for k, ref in enumerate((nbr_ref, index_ref))
    ]
    for copy in [own, *lists]:
        copy.start()
    own.wait()
    copies = [
        pltpu.make_async_copy(own_ref, copies_ref.at[k], sems.at[k]) for k in range(members)
    ]
    for copy in copies:
        copy.start()
    for copy in [*lists, *copies]:
        copy.wait()


def pack_kernel(couplings_ref, packed_ref):
    for m in range(MODES):
        width = couplings_ref.shape[-1]
        packed_ref[:, :, m * width : (m + 1) * width] = couplings_ref[:, m]


def energy_position(spacing):
    energy = lax.axis_index("energy") * lax.axis_size("atom") + lax.axis_index("atom")
    return energy // spacing, energy % spacing


def prepare_kernel(peers, positions, spacing, *refs):
    *tables, occ_ref, packed_ref, left_ref, stack_ref, factor_ref = refs
    for mode, shift in enumerate(SHIFTS):
        for k, sign in enumerate((-1, 1)):
            factor = occ_ref[mode] + float(k)
            if positions:
                at = energy_position(spacing)[0] + sign * (shift // spacing)
                factor = jnp.where(jnp.logical_and(at >= 0, at < positions), factor, 0.0)
            factor_ref[2 * mode + k] = jnp.full(factor_ref.shape[1:], factor, jnp.float32)
    lanes = packed_ref.shape[-1]
    slots = stack_ref.shape[2] // lanes
    rows = left_ref.shape[1] // slots
    columns = left_ref.shape[2] // lanes
    few = left_ref.shape[0] <= FEW
    row_start = pl.multiple_of(lax.axis_index("orb") * rows, rows)

    def prepare(atom, entry):
        count = entry(2, 0)
        for p in range(slots):
            block = entry(1, p)
            stack_ref[atom, :, p * lanes : (p + 1) * lanes] = packed_ref[block]
            part = packed_ref[block, pl.ds(row_start, rows), :]
            first = 0 if few else atom - A_DEV
            place = jnp.where(p < count, entry(0, p) - first, -1)
            for k in range(columns):
                left_ref[atom, p * rows : (p + 1) * rows, k * lanes : (k + 1) * lanes] = jnp.where(
                    place == k, part, jnp.zeros_like(part)
                )

    if peers:
        me = lax.axis_index("atom")
        for k, table_ref in enumerate(tables):
            prepare(me ^ k, lambda row, p, t=table_ref: t[row, p])
    else:
        (table_ref,) = tables
        pl.loop(0, left_ref.shape[0])(lambda a: prepare(a, lambda row, p: table_ref[a, row, p]))


def sigma_kernel(orders, shares, spacing, factor_ref, blocks_ref, left_ref, stack_ref, out_ref, mixed_ref):
    _, atoms, rows, _ = blocks_ref.shape
    orbital = rows * shares
    slots = left_ref.shape[1] // rows
    lanes = MODES * orbital

    def place(mode, k):
        if not orders:
            return [(2 * mode + k) * shares + o for o in range(shares)]
        own, group = energy_position(spacing)
        at = jnp.clip(own + (2 * k - 1) * (SHIFTS[mode] // spacing), 0, len(orders[0]) // shares - 1)
        return [member_place(orders, shares, group, at, o) for o in range(shares)]

    sides = [
        (place(m, 0), place(m, 1), factor_ref[2 * m], factor_ref[2 * m + 1]) for m in range(MODES)
    ]

    def combine(atom, at):
        empty = jnp.zeros((orbital, 2 * orbital), jnp.bfloat16)
        mixed = []
        for low, high, low_scale, high_scale in sides:
            parts = [
                (
                    low_scale * blocks_ref[low[o], atom].astype(jnp.float32)
                    + high_scale * blocks_ref[high[o], atom].astype(jnp.float32)
                ).astype(jnp.bfloat16)
                for o in range(shares)
            ]
            mixed.append(jnp.concatenate(parts, 0))
        mixed_ref[at] = jnp.concatenate(
            [jnp.concatenate([mixed[0], empty], 1), jnp.concatenate([empty, mixed[1]], 1)], 0
        )

    def product(left, first, last):
        mixed = jnp.concatenate([mixed_ref[first + k] for k in range(last - first)], 0)
        return jnp.dot(left, mixed, preferred_element_type=jnp.float32).astype(jnp.bfloat16)

    def finish(atom, half):
        lhs = []
        for c in range(2):
            z = jnp.concatenate(
                [half[:, (2 * m + c) * orbital : (2 * m + c + 1) * orbital] for m in range(MODES)], 1
            )
            lhs.append(jnp.concatenate([z[p * rows : (p + 1) * rows] for p in range(slots)], 1))
        total = lax.dot_general(
            jnp.concatenate(lhs, 0),
            stack_ref[atom],
            (((1,), (1,)), ((), ())),
            preferred_element_type=jnp.float32,
        )
        out_ref[0, atom] = jnp.concatenate([total[:rows], total[rows:]], 1).astype(out_ref.dtype)

    if atoms <= FEW:
        for atom in range(atoms):
            combine(atom, atom)
        halves = []
        for atom in range(atoms):
            first, last = max(atom - A_DEV, 0), min(atom + A_DEV + 1, atoms)
            halves.append(product(left_ref[atom, :, first * lanes : last * lanes], first, last))
        for atom, half in enumerate(halves):
            finish(atom, half)
    else:
        for edge in range(A_DEV):
            for at in (edge, atoms + A_DEV + edge):
                mixed_ref[at] = jnp.zeros(mixed_ref.shape[1:], mixed_ref.dtype)

        @pl.loop(0, atoms)
        def _(atom):
            combine(atom, atom + A_DEV)

        @pl.loop(0, atoms)
        def _(atom):
            mixed = [mixed_ref[atom + k] for k in range(2 * A_DEV + 1)]
            half = jnp.dot(
                left_ref[atom], jnp.concatenate(mixed, 0), preferred_element_type=jnp.float32
            )
            finish(atom, half.astype(jnp.bfloat16))


def body(energies, orb, green_lesser, occupation, coupling_blocks, neighbours, coupling_index, neighbour_count):
    spacing = math.gcd(*SHIFTS)
    _, atoms, rows, width = green_lesser.shape
    slots = neighbours.shape[1]
    orbital = coupling_blocks.shape[-1]
    lanes = MODES * orbital
    peers = lax.axis_size("atom")
    columns, spots = (atoms, atoms) if atoms <= FEW else (2 * A_DEV + 1, atoms + 2 * A_DEV)
    dense = energies <= 2 * max(SHIFTS)
    swap = peers <= 4 and peers & (peers - 1) == 0 and peers == atoms
    params = pltpu.CompilerParams(vmem_limit_bytes=VMEM_LIMIT)

    orders = group_orders(energies, spacing, orb) if dense else ()
    groups = [
        [(k // orb * spacing + c) * orb + k % orb for k in order] for c, order in enumerate(orders)
    ]
    members = len(groups[0]) if dense else 1
    copies, lists = pl.pallas_call(
        copies_kernel,
        out_shape=(
            jax.ShapeDtypeStruct((members, atoms, rows, width), green_lesser.dtype),
            pltpu.VMEM((2, slots), jnp.int32),
        ),
        in_specs=[ANY] * 3,
        out_specs=(ANY, VMEM),
        scratch_shapes=[
            pltpu.VMEM((atoms, rows, width), green_lesser.dtype),
            pltpu.SemaphoreType.DMA((members + 3,)),
        ],
        compiler_params=params,
    )(*map(in_hbm, (green_lesser, neighbours, coupling_index)))
    table = jnp.concatenate([lists, jnp.broadcast_to(neighbour_count[:, None], (1, slots))], 0)
    packed = pl.pallas_call(
        pack_kernel,
        out_shape=pltpu.VMEM((coupling_blocks.shape[0], orbital, lanes), jnp.bfloat16),
        in_specs=[VMEM],
        out_specs=VMEM,
        compiler_params=params,
        cost_estimate=pl.CostEstimate(flops=0, bytes_accessed=4 * 1024 * 1024, transcendentals=0),
    )(in_hbm(coupling_blocks))

    if dense:
        blocks = lax.all_to_all(copies, ALL, 0, 0, axis_index_groups=groups, tiled=True)
    else:
        shares = lax.all_gather(green_lesser[0], "orb")
        blocks = jnp.concatenate(
            [
                lax.ppermute(shares, EA, [(e, e - s) for e in range(energies) if 0 <= e - s < energies])
                for shift in SHIFTS
                for s in (-shift, shift)
            ]
        )
    if swap:
        tables = [table] + [
            lax.ppermute(table, "atom", [(i, i ^ k) for i in range(peers)]) for k in range(1, peers)
        ]
    else:
        tables = [lax.all_gather(table, "atom")]

    left, stack, factors = pl.pallas_call(
        functools.partial(
            prepare_kernel, peers if swap else 0, energies // spacing if dense else 0, spacing
        ),
        out_shape=(
            jax.ShapeDtypeStruct((atoms, slots * rows, columns * lanes), jnp.bfloat16),
            jax.ShapeDtypeStruct((atoms, orbital, slots * lanes), jnp.bfloat16),
            jax.ShapeDtypeStruct((2 * MODES, rows, width), jnp.float32),
        ),
        in_specs=[SMEM] * (len(tables) + 1) + [VMEM],
        out_specs=(VMEM, VMEM, VMEM),
        compiler_params=params,
    )(*tables, occupation, packed)

    return pl.pallas_call(
        functools.partial(sigma_kernel, orders, orb, spacing),
        out_shape=jax.ShapeDtypeStruct(green_lesser.shape, green_lesser.dtype),
        in_specs=[VMEM] * 4,
        out_specs=VMEM,
        scratch_shapes=[pltpu.VMEM((spots, lanes, 2 * lanes), jnp.bfloat16)],
        compiler_params=params,
    )(factors, blocks, left, stack)


def solution(mesh):
    orb = mesh.shape["orb"]
    energies = mesh.shape["energy"] * mesh.shape["atom"]
    placed = (
        P(EA, None, "orb", None),
        P(),
        P(),
        P("atom", None),
        P("atom", None),
        P("atom"),
    )
    return jax.shard_map(
        functools.partial(body, energies, orb),
        mesh=mesh,
        in_specs=placed,
        out_specs=P(EA, None, "orb", None),
        check_vma=False,
    )
```

```python
import functools
import math

import jax
import jax.numpy as jnp
from jax import lax
from jax.experimental import pallas as pl
from jax.experimental.pallas import tpu as pltpu
from jax.sharding import PartitionSpec as P

SHIFTS = (2, 4)
MODES = len(SHIFTS)
A_DEV = 1
EA = ("energy", "atom")
ALL = ("energy", "atom", "orb")
SMEM = pl.BlockSpec(memory_space=pltpu.SMEM)
VMEM = pl.BlockSpec(memory_space=pltpu.VMEM)
ANY = pl.BlockSpec(memory_space=pl.ANY)
VMEM_LIMIT = 32 * 1024 * 1024
MEASURED = (
    (14, 3, 2, 0, 7, 6, 5, 4, 9, 1, 8, 10, 11, 15, 13, 12),
    (3, 2, 1, 0, 7, 11, 4, 6, 8, 10, 15, 9, 5, 14, 13, 12),
)
FEW = 4


def group_orders(energies, spacing, orb):
    if (energies, spacing, orb) == (8, 2, 4):
        return MEASURED
    return (tuple(range(energies // spacing * orb)),) * spacing


def member_place(orders, orb, own_group, energy, share):
    energies = len(orders[0]) // orb
    if energies * len(orders) > 8 or len(orders[0]) > 16:
        return energy * orb + share
    packed = 0
    for g, order in enumerate(orders):
        for e in range(energies):
            packed |= order.index(e * orb + share) << 4 * (g * energies + e)
    packed -= (packed >> 31) << 32
    shift = 4 * (own_group * energies + energy)
    return lax.shift_right_logical(jnp.int32(packed), shift.astype(jnp.int32)) & 15


def in_hbm(array):
    return pltpu.with_memory_space_constraint(array, pltpu.HBM)


def copies_kernel(green_ref, nbr_ref, index_ref, couplings_ref, copies_ref, table_ref, held_ref, own_ref, sems):
    members = copies_ref.shape[0]
    own = pltpu.make_async_copy(green_ref.at[0], own_ref, sems.at[members])
    lists = [
        pltpu.make_async_copy(ref, table_ref.at[k : k + 1], sems.at[members + 1 + k])
        for k, ref in enumerate((nbr_ref, index_ref))
    ]
    lists.append(pltpu.make_async_copy(couplings_ref, held_ref, sems.at[members + 3]))
    for copy in [own, *lists]:
        copy.start()
    own.wait()
    copies = [
        pltpu.make_async_copy(own_ref, copies_ref.at[k], sems.at[k]) for k in range(members)
    ]
    for copy in copies:
        copy.start()
    for copy in [*lists, *copies]:
        copy.wait()


def pack_kernel(couplings_ref, packed_ref):
    for m in range(MODES):
        width = couplings_ref.shape[-1]
        packed_ref[:, :, m * width : (m + 1) * width] = couplings_ref[:, m]


def energy_position(spacing):
    energy = lax.axis_index("energy") * lax.axis_size("atom") + lax.axis_index("atom")
    return energy // spacing, energy % spacing


def preparation(packed_ref, left_ref, stack_ref):
    lanes = packed_ref.shape[-1]
    slots = stack_ref.shape[2] // lanes
    rows = left_ref.shape[1] // slots
    columns = left_ref.shape[2] // lanes
    few = left_ref.shape[0] <= FEW
    row_start = pl.multiple_of(lax.axis_index("orb") * rows, rows)

    def prepare(atom, entry):
        count = entry(2, 0)
        for p in range(slots):
            block = entry(1, p)
            stack_ref[atom, :, p * lanes : (p + 1) * lanes] = packed_ref[block]
            part = packed_ref[block, pl.ds(row_start, rows), :]
            first = 0 if few else atom - A_DEV
            place = jnp.where(p < count, entry(0, p) - first, -1)
            for k in range(columns):
                left_ref[atom, p * rows : (p + 1) * rows, k * lanes : (k + 1) * lanes] = jnp.where(
                    place == k, part, jnp.zeros_like(part)
                )

    return prepare


def prepare_kernel(steps, positions, spacing, *refs):
    *tables, occ_ref, packed_ref, left_ref, stack_ref, factor_ref = refs
    for mode, shift in enumerate(SHIFTS):
        for k, sign in enumerate((-1, 1)):
            factor = occ_ref[mode] + float(k)
            if positions:
                at = energy_position(spacing)[0] + sign * (shift // spacing)
                factor = jnp.where(jnp.logical_and(at >= 0, at < positions), factor, 0.0)
            factor_ref[2 * mode + k] = jnp.full(factor_ref.shape[1:], factor, jnp.float32)
    prepare = preparation(packed_ref, left_ref, stack_ref)
    if steps:
        me = lax.axis_index("atom")
        for k, table_ref in zip(steps, tables):
            prepare(me ^ k, lambda row, p, t=table_ref: t[row, p])
    else:
        (table_ref,) = tables
        pl.loop(0, left_ref.shape[0])(lambda a: prepare(a, lambda row, p: table_ref[a, row, p]))


def complete_kernel(steps, *refs):
    *tables, packed_ref, _, _, left_ref, stack_ref = refs
    me = lax.axis_index("atom")
    prepare = preparation(packed_ref, left_ref, stack_ref)
    for k, table_ref in zip(steps, tables):
        prepare(me ^ k, lambda row, p, t=table_ref: t[row, p])


def sigma_kernel(orders, shares, spacing, factor_ref, blocks_ref, left_ref, stack_ref, out_ref, mixed_ref):
    _, atoms, rows, _ = blocks_ref.shape
    orbital = rows * shares
    slots = left_ref.shape[1] // rows
    lanes = MODES * orbital

    def place(mode, k):
        if not orders:
            return [(2 * mode + k) * shares + o for o in range(shares)]
        own, group = energy_position(spacing)
        at = jnp.clip(own + (2 * k - 1) * (SHIFTS[mode] // spacing), 0, len(orders[0]) // shares - 1)
        return [member_place(orders, shares, group, at, o) for o in range(shares)]

    sides = [
        (place(m, 0), place(m, 1), factor_ref[2 * m], factor_ref[2 * m + 1]) for m in range(MODES)
    ]

    def combine(atom, at):
        empty = jnp.zeros((orbital, 2 * orbital), jnp.bfloat16)
        mixed = []
        for low, high, low_scale, high_scale in sides:
            parts = [
                (
                    low_scale * blocks_ref[low[o], atom].astype(jnp.float32)
                    + high_scale * blocks_ref[high[o], atom].astype(jnp.float32)
                ).astype(jnp.bfloat16)
                for o in range(shares)
            ]
            mixed.append(jnp.concatenate(parts, 0))
        mixed_ref[at] = jnp.concatenate(
            [jnp.concatenate([mixed[0], empty], 1), jnp.concatenate([empty, mixed[1]], 1)], 0
        )

    def product(left, first, last):
        mixed = jnp.concatenate([mixed_ref[first + k] for k in range(last - first)], 0)
        return jnp.dot(left, mixed, preferred_element_type=jnp.float32).astype(jnp.bfloat16)

    def finish(atom, half):
        lhs = []
        for c in range(2):
            z = jnp.concatenate(
                [half[:, (2 * m + c) * orbital : (2 * m + c + 1) * orbital] for m in range(MODES)], 1
            )
            lhs.append(jnp.concatenate([z[p * rows : (p + 1) * rows] for p in range(slots)], 1))
        total = lax.dot_general(
            jnp.concatenate(lhs, 0),
            stack_ref[atom],
            (((1,), (1,)), ((), ())),
            preferred_element_type=jnp.float32,
        )
        out_ref[0, atom] = jnp.concatenate([total[:rows], total[rows:]], 1).astype(out_ref.dtype)

    if atoms <= FEW:
        for atom in range(atoms):
            combine(atom, atom)
        halves = []
        for atom in range(atoms):
            first, last = max(atom - A_DEV, 0), min(atom + A_DEV + 1, atoms)
            halves.append(product(left_ref[atom, :, first * lanes : last * lanes], first, last))
        for atom, half in enumerate(halves):
            finish(atom, half)
    else:
        for edge in range(A_DEV):
            for at in (edge, atoms + A_DEV + edge):
                mixed_ref[at] = jnp.zeros(mixed_ref.shape[1:], mixed_ref.dtype)

        @pl.loop(0, atoms)
        def _(atom):
            combine(atom, atom + A_DEV)

        @pl.loop(0, atoms)
        def _(atom):
            mixed = [mixed_ref[atom + k] for k in range(2 * A_DEV + 1)]
            half = jnp.dot(
                left_ref[atom], jnp.concatenate(mixed, 0), preferred_element_type=jnp.float32
            )
            finish(atom, half.astype(jnp.bfloat16))


def body(energies, orb, green_lesser, occupation, coupling_blocks, neighbours, coupling_index, neighbour_count):
    spacing = math.gcd(*SHIFTS)
    _, atoms, rows, width = green_lesser.shape
    slots = neighbours.shape[1]
    orbital = coupling_blocks.shape[-1]
    lanes = MODES * orbital
    peers = lax.axis_size("atom")
    columns, spots = (atoms, atoms) if atoms <= FEW else (2 * A_DEV + 1, atoms + 2 * A_DEV)
    dense = energies <= 2 * max(SHIFTS)
    swap = peers <= 4 and peers & (peers - 1) == 0 and peers == atoms
    params = pltpu.CompilerParams(vmem_limit_bytes=VMEM_LIMIT)

    orders = group_orders(energies, spacing, orb) if dense else ()
    groups = [
        [(k // orb * spacing + c) * orb + k % orb for k in order] for c, order in enumerate(orders)
    ]
    members = len(groups[0]) if dense else 1
    copies, lists, held = pl.pallas_call(
        copies_kernel,
        out_shape=(
            jax.ShapeDtypeStruct((members, atoms, rows, width), green_lesser.dtype),
            pltpu.VMEM((2, slots), jnp.int32),
            pltpu.VMEM(coupling_blocks.shape, coupling_blocks.dtype),
        ),
        in_specs=[ANY] * 4,
        out_specs=(ANY, VMEM, VMEM),
        scratch_shapes=[
            pltpu.VMEM((atoms, rows, width), green_lesser.dtype),
            pltpu.SemaphoreType.DMA((members + 4,)),
        ],
        compiler_params=params,
    )(*map(in_hbm, (green_lesser, neighbours, coupling_index, coupling_blocks)))
    table = jnp.concatenate([lists, jnp.broadcast_to(neighbour_count[:, None], (1, slots))], 0)
    packed = pl.pallas_call(
        pack_kernel,
        out_shape=pltpu.VMEM((coupling_blocks.shape[0], orbital, lanes), jnp.bfloat16),
        in_specs=[VMEM],
        out_specs=VMEM,
        compiler_params=params,
        cost_estimate=pl.CostEstimate(flops=0, bytes_accessed=4 * 1024 * 1024, transcendentals=0),
    )(held)

    if dense:
        blocks = lax.all_to_all(copies, ALL, 0, 0, axis_index_groups=groups, tiled=True)
    else:
        shares = lax.all_gather(green_lesser[0], "orb")
        blocks = jnp.concatenate(
            [
                lax.ppermute(shares, EA, [(e, e - s) for e in range(energies) if 0 <= e - s < energies])
                for shift in SHIFTS
                for s in (-shift, shift)
            ]
        )
    if swap:
        tables = [table] + [
            lax.ppermute(table, "atom", [(i, i ^ k) for i in range(peers)]) for k in range(1, peers)
        ]
    else:
        tables = [lax.all_gather(table, "atom")]

    early, late = ((0, 1), tuple(range(2, peers))) if swap else ((), ())
    first = tables[: len(early)] if early else tables
    left, stack, factors = pl.pallas_call(
        functools.partial(
            prepare_kernel, early, energies // spacing if dense else 0, spacing
        ),
        out_shape=(
            jax.ShapeDtypeStruct((atoms, slots * rows, columns * lanes), jnp.bfloat16),
            jax.ShapeDtypeStruct((atoms, orbital, slots * lanes), jnp.bfloat16),
            jax.ShapeDtypeStruct((2 * MODES, rows, width), jnp.float32),
        ),
        in_specs=[SMEM] * (len(first) + 1) + [VMEM],
        out_specs=(VMEM, VMEM, VMEM),
        compiler_params=params,
    )(*first, occupation, packed)
    if late:
        count = len(late)
        left, stack = pl.pallas_call(
            functools.partial(complete_kernel, late),
            out_shape=(
                jax.ShapeDtypeStruct(left.shape, left.dtype),
                jax.ShapeDtypeStruct(stack.shape, stack.dtype),
            ),
            in_specs=[SMEM] * count + [VMEM] * 3,
            out_specs=(VMEM, VMEM),
            input_output_aliases={count + 1: 0, count + 2: 1},
            compiler_params=params,
        )(*tables[2:], packed, left, stack)

    return pl.pallas_call(
        functools.partial(sigma_kernel, orders, orb, spacing),
        out_shape=jax.ShapeDtypeStruct(green_lesser.shape, green_lesser.dtype),
        in_specs=[VMEM] * 4,
        out_specs=VMEM,
        scratch_shapes=[pltpu.VMEM((spots, lanes, 2 * lanes), jnp.bfloat16)],
        compiler_params=params,
    )(factors, blocks, left, stack)


def solution(mesh):
    orb = mesh.shape["orb"]
    energies = mesh.shape["energy"] * mesh.shape["atom"]
    placed = (
        P(EA, None, "orb", None),
        P(),
        P(),
        P("atom", None),
        P("atom", None),
        P("atom"),
    )
    return jax.shard_map(
        functools.partial(body, energies, orb),
        mesh=mesh,
        in_specs=placed,
        out_specs=P(EA, None, "orb", None),
        check_vma=False,
    )
```
